32 devices in a mesh: dom: 16 (over z, x, core), snap: 2 (over y).
Axes of the slice: x: 2, y: 2, z: 4, core: 2. Of those that a mesh axis runs over, the one named last changes fastest.
Arguments:
- features: bfloat16 [8, 2048, 256], P('snap', 'dom'), may hold values from -6 to 6
- cotangent: bfloat16 [8, 2048, 256], P('snap', 'dom'), may hold values from -6 to 6
- neighbours: int32 [2048, 16], P('dom'), may hold values from 0 to 2047, as said below
- degrees: int32 [2048], P('dom'), may hold values from 1 to 16
- message_proj: bfloat16 [256, 256], replicated, may hold values from -0.375 to 0.375
- combine_proj: bfloat16 [256, 256], replicated, may hold values from -0.375 to 0.375
- attend_proj: bfloat16 [256, 768], replicated, may hold values from -0.375 to 0.375
- output_proj: bfloat16 [256, 256], replicated, may hold values from -0.375 to 0.375
Outputs:
- grad_features: bfloat16 [8, 2048, 256], P('snap', 'dom')
- grad_message: float32 [256, 256], replicated
- grad_combine: float32 [256, 256], replicated
- grad_attend: float32 [256, 768], replicated
- grad_output: float32 [256, 256], replicated
The draws below stay inside these ranges and needn't reach their ends.
Inputs may be any that keep to these rules, and one draw needn't show every extreme that they name: `neighbours`: a neighbour of a node in rows p * 128 to (p + 1) * 128 - 1 lies in rows p * 128 - 128 to (p + 1) * 128 + 127; slot 0 of the first and of the second node of such a block names the lowest and the highest of those rows that exist.
All inputs are finite; a program needn't handle non-finite values.
Results may differ from the reference program's by a relative error of at most 0.012.
Values may be sent and summed in bfloat16 or wider, within the bound.
A program may use at most 64 MiB of HBM per device.

```python
import math
import jax
import jax.numpy as jnp
from jax import lax

D = 256
HEAD_DIM = 32
SNAPS = 8
DEGREE = 16
NODE_DEV = 128
HALO = 128
NODES = 2048


def draw_neighbours(key, part):
    node_rows = jnp.arange(NODES, dtype=jnp.int32)
    owner_part = node_rows // NODE_DEV
    lowest = jnp.maximum(owner_part * NODE_DEV - HALO, 0)
    highest = jnp.minimum((owner_part + 1) * NODE_DEV + HALO, NODES)
    random_bits = jax.random.randint(key, (NODES, DEGREE), 0, 1 << 30, dtype=jnp.int32)
    picked = lowest[:, None] + random_bits % (highest - lowest)[:, None]
    position = node_rows % NODE_DEV
    slot_index = jnp.arange(DEGREE, dtype=jnp.int32)[None, :]
    picked = jnp.where((position[:, None] == 0) & (slot_index == 0), lowest[:, None], picked)
    picked = jnp.where((position[:, None] == 1) & (slot_index == 0), highest[:, None] - 1, picked)
    return picked.astype(jnp.int32)


def touch_ends(entries, key, least, largest):
    longest = entries.shape.index(max(entries.shape))
    spots = []
    for shift in (0, 1):
        where = [jax.random.randint(jax.random.fold_in(key, axis), (), 0, length) for axis, length in enumerate(entries.shape)]
        where[longest] = (where[longest] + shift) % entries.shape[longest]
        spots.append(tuple(where))
    return entries.at[spots[0]].set(least).at[spots[1]].set(largest)


def levels(own_key, shape, split, low, top_value):
    gain = 1.0
    for dim, blocks in split:
        draws = jax.random.uniform(jax.random.fold_in(jax.random.fold_in(own_key, 6), dim), (blocks,), jnp.float32, low / len(split), top_value / len(split))
        gain = gain * jnp.repeat(jnp.exp(draws), shape[dim] // blocks).reshape((-1,) + (1,) * (len(shape) - 1 - dim))
    return gain


def centred(key, extent, width, most, split=(), held_as=jnp.bfloat16):
    loudness = levels(key, extent, split, -0.22, 0.18) if split else 1.0
    array = jax.random.normal(key, extent, jnp.float32) * width * loudness
    return jnp.minimum(jnp.maximum(array, -most), most).astype(held_as)


def setup_inputs(seed: int = 0) -> dict:
    key_list = jax.random.split(jax.random.key(seed), 9)
    return {
        "features": centred(key_list[0], (SNAPS, NODES, D), 1.0, 6.0, ((0, 2), (1, 16))),
        "cotangent": centred(key_list[1], (SNAPS, NODES, D), 1.0, 6.0, ((0, 2), (1, 16))),
        "neighbours": draw_neighbours(jax.random.fold_in(key_list[8], 71), 0),
        "degrees": touch_ends(jax.random.randint(key_list[3], (NODES,), 1, DEGREE + 1), jax.random.fold_in(key_list[3], 1), 1, DEGREE).astype(jnp.int32),
        "message_proj": centred(key_list[4], (D, D), D ** -0.5, 0.375),
        "combine_proj": centred(key_list[5], (D, D), D ** -0.5, 0.375),
        "attend_proj": centred(key_list[6], (D, 3 * D), D ** -0.5, 0.375),
        "output_proj": centred(key_list[7], (D, D), D ** -0.5, 0.375),
    }


def silu_slope(inputs_pre):
    logistic = jax.nn.sigmoid(inputs_pre)
    return logistic * (1.0 + inputs_pre * (1.0 - logistic))

def edge_inputs(message_rows, own_block, neighbour_block, degree_block):
    gathered = jnp.take(message_rows, neighbour_block, axis=0)
    before = gathered + own_block.astype(jnp.float32)[:, None, :]
    slot_index = jnp.arange(neighbour_block.shape[1], dtype=jnp.int32)
    used = (slot_index[None, :] < degree_block[:, None]).astype(jnp.float32)
    weights = used / degree_block.astype(jnp.float32)[:, None]
    return (before, weights)

def spatial_forward(own_rows, message_rows, neighbour_index, degrees, combine_proj, block_rows):
    node_count = own_rows.shape[0]

    def per_block(block_index):
        offset = block_index * block_rows
        own_block = lax.dynamic_slice_in_dim(own_rows, offset, block_rows, 0)
        neighbour_block = lax.dynamic_slice_in_dim(neighbour_index, offset, block_rows, 0)
        degree_block = lax.dynamic_slice_in_dim(degrees, offset, block_rows, 0)
        before, weights = edge_inputs(message_rows, own_block, neighbour_block, degree_block)
        return lax.optimization_barrier(jnp.sum(jax.nn.silu(before) * weights[:, :, None], axis=1))
    combined = lax.map(per_block, jnp.arange(node_count // block_rows, dtype=jnp.int32))
    combined = combined.reshape(node_count, -1).astype(jnp.bfloat16)
    spatial = own_rows.astype(jnp.float32) + jnp.dot(combined, combine_proj, preferred_element_type=jnp.float32)
    return (combined, spatial.astype(jnp.bfloat16))

def spatial_backward(own_rows, message_rows, neighbour_index, degrees, grad_spatial, combine_proj, block_rows):
    node_count = own_rows.shape[0]
    feature_width = own_rows.shape[1]
    grad_combined = jnp.dot(grad_spatial, combine_proj.T, preferred_element_type=jnp.float32)

    def per_block(totals, block_index):
        offset = block_index * block_rows
        own_block = lax.dynamic_slice_in_dim(own_rows, offset, block_rows, 0)
        neighbour_block = lax.dynamic_slice_in_dim(neighbour_index, offset, block_rows, 0)
        degree_block = lax.dynamic_slice_in_dim(degrees, offset, block_rows, 0)
        grad_block = lax.dynamic_slice_in_dim(grad_combined, offset, block_rows, 0)
        before, weights = edge_inputs(message_rows, own_block, neighbour_block, degree_block)
        grad_before = grad_block[:, None, :] * weights[:, :, None] * silu_slope(before)
        totals = totals.at[neighbour_block.reshape(-1)].add(grad_before.reshape(-1, feature_width))
        return (totals, lax.optimization_barrier(jnp.sum(grad_before, axis=1)))
    start_rows = jnp.zeros((message_rows.shape[0], feature_width), jnp.float32)
    grad_rows, self_terms = lax.scan(per_block, start_rows, jnp.arange(node_count // block_rows, dtype=jnp.int32))
    return (grad_rows, self_terms.reshape(node_count, feature_width))

def temporal_block(spat_block, cot_block, attend_proj, output_proj):
    snap_count, node_count, feature_width = spat_block.shape
    head_count = feature_width // HEAD_DIM
    row_count = snap_count * node_count
    flat_spat = spat_block.reshape(row_count, feature_width)
    flat_cot = cot_block.reshape(row_count, feature_width)
    projected = jnp.dot(flat_spat, attend_proj, preferred_element_type=jnp.float32)
    projected = projected.reshape(snap_count, node_count, 3, head_count, HEAD_DIM)
    query_rows = projected[:, :, 0]
    key_rows = projected[:, :, 1]
    value_rows = projected[:, :, 2]
    inverse_root = 1.0 / math.sqrt(HEAD_DIM)
    precise = lax.Precision.HIGHEST
    scores = jnp.einsum('snhe,rnhe->nhsr', query_rows, key_rows, precision=precise) * inverse_root
    exponent = jnp.exp(scores)
    soft_weights = exponent / lax.optimization_barrier(jnp.sum(exponent, axis=-1, keepdims=True))
    attended = jnp.einsum('nhsr,rnhe->snhe', soft_weights, value_rows, precision=precise)
    attended = attended.reshape(row_count, feature_width).astype(jnp.bfloat16)
    grad_output = jnp.dot(attended.T, flat_cot, preferred_element_type=jnp.float32)
    grad_attended = jnp.dot(flat_cot, output_proj.T, preferred_element_type=jnp.float32)
    grad_attended = grad_attended.reshape(snap_count, node_count, head_count, HEAD_DIM)
    grad_soft = jnp.einsum('snhe,rnhe->nhsr', grad_attended, value_rows, precision=precise)
    grad_value = jnp.einsum('nhsr,snhe->rnhe', soft_weights, grad_attended, precision=precise)
    grad_score = soft_weights * (grad_soft - lax.optimization_barrier(jnp.sum(soft_weights * grad_soft, axis=-1, keepdims=True))) * inverse_root
    grad_query = jnp.einsum('nhsr,rnhe->snhe', grad_score, key_rows, precision=precise)
    grad_key = jnp.einsum('nhsr,snhe->rnhe', grad_score, query_rows, precision=precise)
    grad_three = jnp.stack([grad_query, grad_key, grad_value], axis=2)
    grad_three = grad_three.reshape(row_count, 3 * feature_width).astype(jnp.bfloat16)
    grad_attend = jnp.dot(flat_spat.T, grad_three, preferred_element_type=jnp.float32)
    grad_spatial = flat_cot.astype(jnp.float32) + jnp.dot(grad_three, attend_proj.T, preferred_element_type=jnp.float32)
    grad_spatial = grad_spatial.astype(jnp.bfloat16).reshape(snap_count, node_count, feature_width)
    return (grad_spatial, grad_attend, grad_output)

def reference(features, cotangent, neighbours, degrees, message_proj, combine_proj, attend_proj, output_proj):
    block_rows = NODE_DEV
    message_list = []
    combined_list = []
    spatial_list = []
    for snapshot in range(SNAPS):
        message_rows = jnp.dot(features[snapshot], message_proj, preferred_element_type=jnp.float32)
        combined, spatial = spatial_forward(features[snapshot], message_rows, neighbours, degrees, combine_proj, block_rows)
        message_list.append(message_rows)
        combined_list.append(combined)
        spatial_list.append(spatial)
    spatial_all = jnp.stack(spatial_list)

    def temporal_step(totals, block_index):
        offset = block_index * NODE_DEV
        spat_block = lax.dynamic_slice_in_dim(spatial_all, offset, NODE_DEV, 1)
        cot_block = lax.dynamic_slice_in_dim(cotangent, offset, NODE_DEV, 1)
        grad_block, grad_attend, grad_output = temporal_block(spat_block, cot_block, attend_proj, output_proj)
        buffer = lax.dynamic_update_slice_in_dim(totals[2], grad_block, offset, 1)
        return ((totals[0] + grad_attend, totals[1] + grad_output, buffer), None)
    start_totals = (jnp.zeros((D, 3 * D), jnp.float32), jnp.zeros((D, D), jnp.float32), jnp.zeros((SNAPS, NODES, D), jnp.bfloat16))
    totals, unused_out = lax.scan(temporal_step, start_totals, jnp.arange(NODES // NODE_DEV, dtype=jnp.int32))
    raw_attend, raw_output, grad_spatial_all = totals
    raw_message = jnp.zeros((D, D), jnp.float32)
    raw_combine = jnp.zeros((D, D), jnp.float32)
    grad_list = []
    for snapshot in range(SNAPS):
        grad_spatial = grad_spatial_all[snapshot]
        raw_combine = raw_combine + jnp.dot(combined_list[snapshot].T, grad_spatial, preferred_element_type=jnp.float32)
        grad_rows, self_terms = spatial_backward(features[snapshot], message_list[snapshot], neighbours, degrees, grad_spatial, combine_proj, block_rows)
        grad_rows = grad_rows.astype(jnp.bfloat16)
        raw_message = raw_message + jnp.dot(features[snapshot].T, grad_rows, preferred_element_type=jnp.float32)
        grad_here = grad_spatial.astype(jnp.float32) + self_terms
        grad_here = grad_here + jnp.dot(grad_rows, message_proj.T, preferred_element_type=jnp.float32)
        grad_list.append(grad_here.astype(jnp.bfloat16))
    factor = 1.0 / math.sqrt(SNAPS * NODES)
    grad_features = jnp.stack(grad_list)
    return (grad_features, raw_message * factor, raw_combine * factor, raw_attend * factor, raw_output * factor)
```

```python
import functools
import math

import jax
import jax.numpy as jnp
from jax import lax
from jax.experimental import pallas as pl
from jax.experimental.pallas import tpu as pltpu
from jax.sharding import PartitionSpec as P

HEAD_DIM = 32
SNAPS = 8
HALO = 128
LOW = 4
F32 = jnp.float32
BF16 = jnp.bfloat16


def dot(a, b):
    return jnp.dot(a, b, preferred_element_type=F32)


def dot_t(a, b):
    return lax.dot_general(a, b, (((1,), (1,)), ((), ())), preferred_element_type=F32)


def t_dot(a, b):
    return lax.dot_general(a, b, (((0,), (0,)), ((), ())), preferred_element_type=F32)


def remote(src, dst, send, recv, device):
    return pltpu.make_async_remote_copy(
        src_ref=src,
        dst_ref=dst,
        send_sem=send,
        recv_sem=recv,
        device_id=device,
        device_id_type=pl.DeviceIdType.MESH,
    )


class Reduce:
    def __init__(self, dims, base, rows, part, fin, first, second, sems):
        self.doms, self.snaps, self.me_d, self.me_s = dims
        self.low = LOW if self.doms % LOW == 0 else 1
        self.high = self.doms // self.low
        self.group = self.low * self.snaps
        self.piece = rows // self.group
        self.base = base
        self.part, self.fin, self.first, self.second = part, fin, first, second
        self.sems = sems
        self.hi = self.me_d // self.low
        self.mine = self.me_s * self.low + self.me_d % self.low
        self.sent = []

    def member(self, t):
        return (self.hi * self.low + t % self.low, t // self.low)

    def rows_of(self, t):
        return pl.ds(pl.multiple_of(self.base + t * self.piece, 16), self.piece)

    def start(self):
        s1, r1 = self.sems[0], self.sems[1]
        for d in range(1, self.group):
            t = (self.mine + d) % self.group
            copy = remote(
                self.part.at[self.rows_of(t)],
                self.first.at[d - 1],
                s1.at[d - 1],
                r1.at[d - 1],
                self.member(t),
            )
            copy.start()
            self.sent.append(copy)
        self.one = list(self.sent)

    def middle(self):
        s2, r2 = self.sems[2], self.sems[3]
        total = self.part[self.rows_of(self.mine), :].astype(F32)
        for d in range(1, self.group):
            self.one[d - 1].wait_recv()
            total = total + self.first[d - 1].astype(F32)
        self.second[self.hi] = total.astype(BF16)
        for d in range(1, self.high):
            a = (self.hi + d) % self.high
            copy = remote(
                self.second.at[self.hi],
                self.second.at[self.hi],
                s2.at[d - 1],
                r2.at[d - 1],
                (a * self.low + self.me_d % self.low, self.me_s),
            )
            copy.start()
            self.sent.append(copy)

    def spread(self):
        s2, r2, s3, r3 = self.sems[2:]
        for d in range(1, self.high):
            a = (self.hi + self.high - d) % self.high
            remote(
                self.second.at[a],
                self.second.at[a],
                s2.at[d - 1],
                r2.at[d - 1],
                (a * self.low + self.me_d % self.low, self.me_s),
            ).wait_recv()
        total = self.second[0].astype(F32)
        for a in range(1, self.high):
            total = total + self.second[a].astype(F32)
        self.fin[self.rows_of(self.mine), :] = total.astype(BF16)
        for d in range(1, self.group):
            t = (self.mine + d) % self.group
            copy = remote(
                self.fin.at[self.rows_of(self.mine)],
                self.fin.at[self.rows_of(self.mine)],
                s3.at[d - 1],
                r3.at[d - 1],
                self.member(t),
            )
            copy.start()
            self.sent.append(copy)

    def finish(self):
        s3, r3 = self.sems[4:]
        for d in range(1, self.group):
            t = (self.mine + self.group - d) % self.group
            remote(
                self.fin.at[self.rows_of(t)],
                self.fin.at[self.rows_of(t)],
                s3.at[d - 1],
                r3.at[d - 1],
                self.member(t),
            ).wait_recv()
        for copy in self.sent:
            copy.wait_send()


def kernel(
    doms, snaps,
    feat, cot, nb, nbt, deg, wm, wc, wa, wo,
    gfeat, wout,
    ext, cat, oh, oht, wb, bef, slope, comb, spat, spsw, cosw,
    q, k, v, ga, gq, gk, gv, att, sc, gs, gsw, gsp, gb, grow, ownf, selff, ghl, ghr,
    part, first_a, second_a, first_b, second_b, fin,
    halo_s, halo_r, gho_s, gho_r, cot_s, cot_r, spa_s, spa_r, gra_s, gra_r, *red,
):
    local, nodes, width = feat.shape
    degree = nb.shape[1]
    reach = nodes + 2 * HALO
    share = nodes // snaps
    me_d, me_s = lax.axis_index("dom"), lax.axis_index("snap")
    dims = (doms, snaps, me_d, me_s)
    left, right = (me_d + doms - 1) % doms, (me_d + 1) % doms
    red_a = Reduce(dims, 0, 4 * width, part, fin, first_a, second_a, red[:6])
    red_b = Reduce(dims, 4 * width, 2 * width, part, fin, first_b, second_b, red[6:])

    barrier = pltpu.get_barrier_semaphore()

    def greet(device):
        pl.semaphore_signal(
            barrier, inc=1, device_id=device, device_id_type=pl.DeviceIdType.MESH
        )

    greet((left, me_s))
    greet((right, me_s))
    for d in range(1, red_a.group):
        greet(red_a.member((red_a.mine + d) % red_a.group))
    for d in range(1, red_a.high):
        a = (red_a.hi + d) % red_a.high
        greet((a * red_a.low + me_d % red_a.low, me_s))
    pl.semaphore_wait(barrier, red_a.group + red_a.high)

    def to_right(s):
        return remote(feat.at[s], ext.at[s, pl.ds(0, HALO)], halo_s.at[0, s], halo_r.at[0, s], (right, me_s))

    def to_left(s):
        return remote(
            feat.at[s], ext.at[s, pl.ds(reach - HALO, HALO)], halo_s.at[1, s], halo_r.at[1, s], (left, me_s)
        )

    has_left, has_right = me_d > 0, me_d < doms - 1
    for s in range(local):
        pl.when(has_right)(lambda s=s: to_right(s).start())
        pl.when(has_left)(lambda s=s: to_left(s).start())

    def my_slots():
        return pl.ds(me_s * local, local)

    def share_of(p):
        return pl.ds(pl.multiple_of(p * share, share), share)

    cot_out = []
    for d in range(1, snaps):
        p = (me_s + d) % snaps
        copy = remote(
            cot.at[:, share_of(p)], cosw.at[my_slots()], cot_s.at[d - 1], cot_r.at[d - 1], (me_d, p)
        )
        copy.start()
        cot_out.append(copy)
    for s in range(local):
        cosw[me_s * local + s] = cot[s, share_of(me_s), :]

    @pl.when(jnp.logical_not(has_left))
    def _():
        ext[:, pl.ds(0, HALO), :] = jnp.zeros((local, HALO, width), BF16)
        ghl[...] = jnp.zeros(ghl.shape, BF16)

    @pl.when(jnp.logical_not(has_right))
    def _():
        ext[:, pl.ds(reach - HALO, HALO), :] = jnp.zeros((local, HALO, width), BF16)
        ghr[...] = jnp.zeros(ghr.shape, BF16)

    ext[:, pl.ds(HALO, nodes), :] = feat[...]

    first_row = me_d * nodes - HALO
    index = nb[...] - first_row
    index_t = nbt[...] - first_row
    lanes = lax.broadcasted_iota(jnp.int32, (nodes, reach), 1)
    subs = lax.broadcasted_iota(jnp.int32, (reach, nodes), 0)
    eye = jnp.where(
        lax.broadcasted_iota(jnp.int32, (nodes, nodes), 0)
        == lax.broadcasted_iota(jnp.int32, (nodes, nodes), 1),
        1.0,
        0.0,
    ).astype(BF16)
    counts = deg[...]
    inverse = 1.0 / counts.astype(F32)
    for j in range(degree):
        at = pl.ds(j * nodes, nodes)
        oh[at, pl.ds(0, reach)] = jnp.where(lanes == index[:, j : j + 1], 1.0, 0.0).astype(BF16)
        oh[at, pl.ds(reach, nodes)] = eye
        oht[pl.ds(0, reach), at] = jnp.where(subs == index_t[j : j + 1, :], 1.0, 0.0).astype(BF16)
        oht[pl.ds(reach, nodes), at] = eye
        wb[at, :] = jnp.broadcast_to(jnp.where(counts > j, inverse, 0.0), (nodes, 128))

    block = 32
    spa_out = []
    for s in range(local):
        pl.when(has_left)(lambda s=s: to_right(s).wait_recv())
        pl.when(has_right)(lambda s=s: to_left(s).wait_recv())
        cat[pl.ds(0, reach), :] = dot(ext[s], wm[...]).astype(BF16)
        cat[pl.ds(reach, nodes), :] = feat[s]
        bef[...] = dot(oh[...], cat[...])

        def forward(c, carry, s=s):
            total = jnp.zeros((block, width), F32)
            for j in range(degree):
                at = pl.ds(pl.multiple_of(j * nodes + c * block, block), block)
                x = bef[at, :]
                w = wb[at, :]
                w = jnp.concatenate([w] * (width // 128), axis=1)
                g = 0.5 * jnp.tanh(0.5 * x) + 0.5
                y = x * g
                total = total + w * y
                slope[s, at, :] = (w * (g + y * (1.0 - g))).astype(BF16)
            comb[s, pl.ds(pl.multiple_of(c * block, block), block), :] = total.astype(BF16)
            return carry

        lax.fori_loop(0, nodes // block, forward, 0)
        spat[s] = (feat[s].astype(F32) + dot(comb[s], wc[...])).astype(BF16)
        for d in range(1, snaps):
            p = (me_s + d) % snaps
            copy = remote(
                spat.at[s, share_of(p)],
                spsw.at[me_s * local + s],
                spa_s.at[s, d - 1],
                spa_r.at[s, d - 1],
                (me_d, p),
            )
            copy.start()
            spa_out.append((s, d, copy))
        spsw[me_s * local + s] = spat[s, share_of(me_s), :]

    rows = SNAPS * share
    for copy in cot_out:
        copy.wait_recv()
    flat_cot = cosw[...].reshape(rows, width)
    ga[...] = dot_t(flat_cot, wo[...])
    for s, d, copy in spa_out:
        copy.wait_recv()
    flat_spat = spsw[...].reshape(rows, width)
    q[...] = dot(flat_spat, wa[:, 0:width])
    k[...] = dot(flat_spat, wa[:, width : 2 * width])
    v[...] = dot(flat_spat, wa[:, 2 * width : 3 * width])
    root = 1.0 / math.sqrt(HEAD_DIM)
    heads = jnp.where(
        lax.broadcasted_iota(jnp.int32, (width, width), 0) // HEAD_DIM
        == lax.broadcasted_iota(jnp.int32, (width, width), 1) // HEAD_DIM,
        1.0,
        0.0,
    ).astype(BF16)

    def pairs(s, carry):
        at = pl.ds(pl.multiple_of(s * share, share), share)
        out = pl.ds(pl.multiple_of(s * rows, rows), rows)
        mine = q[at, :] * root
        other = ga[at, :]
        sc[out, :] = dot(
            (k[...].reshape(SNAPS, share, width) * mine[None]).astype(BF16).reshape(rows, width), heads
        )
        gs[out, :] = dot(
            (v[...].reshape(SNAPS, share, width) * other[None]).astype(BF16).reshape(rows, width), heads
        )
        return carry

    lax.fori_loop(0, SNAPS, pairs, 0)

    small = 8

    def attend(c, carry):
        def at(s):
            return pl.ds(pl.multiple_of(s * share + c * small, small), small)

        gk_sum = [jnp.zeros((small, width), F32)] * SNAPS
        gv_sum = [jnp.zeros((small, width), F32)] * SNAPS
        for s in range(SNAPS):
            e = [jnp.exp(sc[at(s * SNAPS + r), :]) for r in range(SNAPS)]
            norm = 1.0 / sum(e[1:], e[0])
            w = [x * norm for x in e]
            g = [gs[at(s * SNAPS + r), :] for r in range(SNAPS)]
            prods = [x * y for x, y in zip(w, g)]
            mean = sum(prods[1:], prods[0])
            mine, other = q[at(s), :], ga[at(s), :]
            att_sum = jnp.zeros((small, width), F32)
            gq_sum = jnp.zeros((small, width), F32)
            for r in range(SNAPS):
                t = w[r] * (g[r] - mean)
                att_sum = att_sum + w[r] * v[at(r), :]
                gq_sum = gq_sum + t * k[at(r), :]
                gk_sum[r] = gk_sum[r] + t * mine
                gv_sum[r] = gv_sum[r] + w[r] * other
            att[at(s), :] = att_sum
            gq[at(s), :] = gq_sum * root
        for r in range(SNAPS):
            gk[at(r), :] = gk_sum[r] * root
            gv[at(r), :] = gv_sum[r]
        return carry

    lax.fori_loop(0, share // small, attend, 0)

    g3 = [gq[...].astype(BF16), gk[...].astype(BF16), gv[...].astype(BF16)]
    back = flat_cot.astype(F32)
    for n in range(3):
        back = back + dot_t(g3[n], wa[:, n * width : (n + 1) * width])
    gsw[...] = back.astype(BF16).reshape(SNAPS, share, width)
    gra_out = []
    for d in range(1, snaps):
        p = (me_s + d) % snaps
        copy = remote(
            gsw.at[pl.ds(p * local, local)],
            gsp.at[:, share_of(me_s)],
            gra_s.at[d - 1],
            gra_r.at[d - 1],
            (me_d, p),
        )
        copy.start()
        gra_out.append(copy)
    for s in range(local):
        gsp[s, share_of(me_s), :] = gsw[me_s * local + s]
    part[pl.ds(0, width), :] = t_dot(att[...].astype(BF16), flat_cot).astype(BF16)
    for n in range(3):
        part[pl.ds((n + 1) * width, width), :] = t_dot(flat_spat, g3[n]).astype(BF16)
    red_a.start()
    for d in range(1, snaps):
        p = (me_s + snaps - d) % snaps
        remote(
            gsw.at[pl.ds(p * local, local)],
            gsp.at[:, share_of(p)],
            gra_s.at[d - 1],
            gra_r.at[d - 1],
            (me_d, p),
        ).wait_recv()

    def ghost_left(s):
        return remote(grow.at[s, pl.ds(0, HALO)], ghr.at[s], gho_s.at[0, s], gho_r.at[0, s], (left, me_s))

    def ghost_right(s):
        return remote(
            grow.at[s, pl.ds(reach - HALO, HALO)], ghl.at[s], gho_s.at[1, s], gho_r.at[1, s], (right, me_s)
        )

    part[pl.ds(4 * width, width), :] = t_dot(
        comb[...].reshape(local * nodes, width), gsp[...].reshape(local * nodes, width)
    ).astype(BF16)
    for s in range(local):
        bef[pl.ds(0, nodes), :] = dot_t(gsp[s], wc[...])

        def backward(c, carry, s=s):
            gc = bef[pl.ds(pl.multiple_of(c * block, block), block), :]
            for j in range(degree):
                at = pl.ds(pl.multiple_of(j * nodes + c * block, block), block)
                gb[at, :] = (gc * slope[s, at, :].astype(F32)).astype(BF16)
            return carry

        lax.fori_loop(0, nodes // block, backward, 0)
        sums = dot(oht[...], gb[...])
        grow[s] = sums[:reach].astype(BF16)
        ownf[s] = sums[HALO : HALO + nodes]
        selff[s] = sums[reach:]
        pl.when(has_left)(lambda s=s: ghost_left(s).start())
        pl.when(has_right)(lambda s=s: ghost_right(s).start())
        if s == local // 2:
            red_a.middle()
    part[pl.ds(5 * width, width), :] = t_dot(
        ext[...].reshape(local * reach, width), grow[...].reshape(local * reach, width)
    ).astype(BF16)
    red_b.start()
    red_a.spread()
    for s in range(local):
        pl.when(has_right)(lambda s=s: ghost_left(s).wait_recv())
        pl.when(has_left)(lambda s=s: ghost_right(s).wait_recv())
        if s == local // 2:
            red_b.middle()
        own = ownf[s] + ghl[s].astype(F32) + ghr[s].astype(F32)
        here = gsp[s].astype(F32) + selff[s] + dot_t(own.astype(BF16), wm[...])
        gfeat[s] = here.astype(BF16)
    red_b.spread()
    red_a.finish()
    red_b.finish()
    wout[...] = fin[...]
    for s in range(local):
        @pl.when(has_right)
        def _(s=s):
            to_right(s).wait_send()
            ghost_right(s).wait_send()

        @pl.when(has_left)
        def _(s=s):
            to_left(s).wait_send()
            ghost_left(s).wait_send()
    for copy in cot_out + [c for _, _, c in spa_out] + gra_out:
        copy.wait_send()


def body(doms, snaps, features, cotangent, neighbours, degrees, message_proj, combine_proj, attend_proj, output_proj):
    local, nodes, width = features.shape
    degree = neighbours.shape[1]
    reach = nodes + 2 * HALO
    share = nodes // snaps
    rows = SNAPS * share
    low = LOW if doms % LOW == 0 else 1
    high, group = doms // low, low * snaps
    dma = pltpu.SemaphoreType.DMA
    vmem = pltpu.VMEM

    def reduce_sems():
        g, h = (max(group - 1, 1),), (max(high - 1, 1),)
        return [dma(g), dma(g), dma(h), dma(h), dma(g), dma(g)]

    peers = max(snaps - 1, 1)
    gfeat, wout = pl.pallas_call(
        functools.partial(kernel, doms, snaps),
        out_shape=(
            jax.ShapeDtypeStruct(features.shape, BF16),
            jax.ShapeDtypeStruct((6 * width, width), BF16),
        ),
        in_specs=[pl.BlockSpec(memory_space=pltpu.VMEM)] * 9,
        out_specs=[pl.BlockSpec(memory_space=pltpu.VMEM)] * 2,
        scratch_shapes=[
            vmem((local, reach, width), BF16),
            vmem((reach + nodes, width), BF16),
            vmem((degree * nodes, reach + nodes), BF16),
            vmem((reach + nodes, degree * nodes), BF16),
            vmem((degree * nodes, 128), F32),
            vmem((degree * nodes, width), F32),
            vmem((local, degree * nodes, width), BF16),
            vmem((local, nodes, width), BF16),
            vmem((local, nodes, width), BF16),
            vmem((SNAPS, share, width), BF16),
            vmem((SNAPS, share, width), BF16),
            *[vmem((rows, width), F32)] * 8,
            vmem((SNAPS * rows, width), F32),
            vmem((SNAPS * rows, width), F32),
            vmem((SNAPS, share, width), BF16),
            vmem((local, nodes, width), BF16),
            vmem((degree * nodes, width), BF16),
            vmem((local, reach, width), BF16),
            vmem((local, nodes, width), F32),
            vmem((local, nodes, width), F32),
            vmem((local, HALO, width), BF16),
            vmem((local, HALO, width), BF16),
            vmem((6 * width, width), BF16),
            vmem((group - 1, 4 * width // group, width), BF16),
            vmem((high, 4 * width // group, width), BF16),
            vmem((group - 1, 2 * width // group, width), BF16),
            vmem((high, 2 * width // group, width), BF16),
            vmem((6 * width, width), BF16),
            dma((2, local)),
            dma((2, local)),
            dma((2, local)),
            dma((2, local)),
            dma((peers,)),
            dma((peers,)),
            dma((local, peers)),
            dma((local, peers)),
            dma((peers,)),
            dma((peers,)),
            *reduce_sems(),
            *reduce_sems(),
        ],
        compiler_params=pltpu.CompilerParams(
            collective_id=0, has_side_effects=True, vmem_limit_bytes=56 * 2**20
        ),
    )(
        features, cotangent, neighbours, neighbours.T, degrees.reshape(nodes, 1),
        message_proj, combine_proj, attend_proj, output_proj,
    )
    factor = 1.0 / math.sqrt(SNAPS * doms * nodes)
    block = [wout[n * width : (n + 1) * width].astype(F32) * factor for n in range(6)]
    return (gfeat, block[5], block[4], jnp.concatenate(block[1:4], axis=1), block[0])


def solution(mesh):
    in_specs = (
        P("snap", "dom", None),
        P("snap", "dom", None),
        P("dom", None),
        P("dom"),
        P(),
        P(),
        P(),
        P(),
    )
    out_specs = (P("snap", "dom", None), P(), P(), P(), P())
    return jax.shard_map(
        functools.partial(body, mesh.shape["dom"], mesh.shape["snap"]),
        mesh=mesh,
        in_specs=in_specs,
        out_specs=out_specs,
        check_vma=False,
    )
```

```python
import functools
import math

import jax
import jax.numpy as jnp
from jax import lax
from jax.experimental import pallas as pl
from jax.experimental.pallas import tpu as pltpu
from jax.sharding import PartitionSpec as P

HEAD_DIM = 32
SNAPS = 8
HALO = 128
LOW = 4
F32 = jnp.float32
BF16 = jnp.bfloat16


def dot(a, b):
    return jnp.dot(a, b, preferred_element_type=F32)


def dot_t(a, b):
    return lax.dot_general(a, b, (((1,), (1,)), ((), ())), preferred_element_type=F32)


def t_dot(a, b):
    return lax.dot_general(a, b, (((0,), (0,)), ((), ())), preferred_element_type=F32)


def remote(src, dst, send, recv, device):
    return pltpu.make_async_remote_copy(
        src_ref=src,
        dst_ref=dst,
        send_sem=send,
        recv_sem=recv,
        device_id=device,
        device_id_type=pl.DeviceIdType.MESH,
    )


class Reduce:
    def __init__(self, dims, base, rows, part, fin, first, second, sems):
        self.doms, self.snaps, self.me_d, self.me_s = dims
        self.low = LOW if self.doms % LOW == 0 else 1
        self.high = self.doms // self.low
        self.group = self.low * self.snaps
        self.piece = rows // self.group
        self.base = base
        self.part, self.fin, self.first, self.second = part, fin, first, second
        self.sems = sems
        self.hi = self.me_d // self.low
        self.mine = self.me_s * self.low + self.me_d % self.low
        self.sent = []

    def member(self, t):
        return (self.hi * self.low + t % self.low, t // self.low)

    def rows_of(self, t):
        return pl.ds(pl.multiple_of(self.base + t * self.piece, 16), self.piece)

    def start(self):
        s1, r1 = self.sems[0], self.sems[1]
        for d in range(1, self.group):
            t = (self.mine + d) % self.group
            copy = remote(
                self.part.at[self.rows_of(t)],
                self.first.at[d - 1],
                s1.at[d - 1],
                r1.at[d - 1],
                self.member(t),
            )
            copy.start()
            self.sent.append(copy)
        self.one = list(self.sent)

    def middle(self):
        s2, r2 = self.sems[2], self.sems[3]
        total = self.part[self.rows_of(self.mine), :].astype(F32)
        for d in range(1, self.group):
            self.one[d - 1].wait_recv()
            total = total + self.first[d - 1].astype(F32)
        self.second[self.hi] = total.astype(BF16)
        for d in range(1, self.high):
            a = (self.hi + d) % self.high
            copy = remote(
                self.second.at[self.hi],
                self.second.at[self.hi],
                s2.at[d - 1],
                r2.at[d - 1],
                (a * self.low + self.me_d % self.low, self.me_s),
            )
            copy.start()
            self.sent.append(copy)

    def spread(self):
        s2, r2, s3, r3 = self.sems[2:]
        for d in range(1, self.high):
            a = (self.hi + self.high - d) % self.high
            remote(
                self.second.at[a],
                self.second.at[a],
                s2.at[d - 1],
                r2.at[d - 1],
                (a * self.low + self.me_d % self.low, self.me_s),
            ).wait_recv()
        total = self.second[0].astype(F32)
        for a in range(1, self.high):
            total = total + self.second[a].astype(F32)
        self.fin[self.rows_of(self.mine), :] = total.astype(BF16)
        for d in range(1, self.group):
            t = (self.mine + d) % self.group
            copy = remote(
                self.fin.at[self.rows_of(self.mine)],
                self.fin.at[self.rows_of(self.mine)],
                s3.at[d - 1],
                r3.at[d - 1],
                self.member(t),
            )
            copy.start()
            self.sent.append(copy)

    def finish(self):
        s3, r3 = self.sems[4:]
        for d in range(1, self.group):
            t = (self.mine + self.group - d) % self.group
            remote(
                self.fin.at[self.rows_of(t)],
                self.fin.at[self.rows_of(t)],
                s3.at[d - 1],
                r3.at[d - 1],
                self.member(t),
            ).wait_recv()
        for copy in self.sent:
            copy.wait_send()


def kernel(
    doms, snaps,
    feat, cot, nb, deg, wm, wc, wa, wo,
    gfeat, wout,
    ext, cat, oh, oht, wb, slope, comb, spat, spsw, cosw,
    q, k, v, ga, gq, gk, gv, att, gsw, gsp, grow, ownf, selff, ghl, ghr,
    part, first_a, second_a, first_b, second_b, first_c, second_c, fin,
    halo_s, halo_r, gho_s, gho_r, cot_s, cot_r, spa_s, spa_r, gra_s, gra_r, *red,
):
    local, nodes, width = feat.shape
    degree = nb.shape[1]
    reach = nodes + 2 * HALO
    share = nodes // snaps
    me_d, me_s = lax.axis_index("dom"), lax.axis_index("snap")
    dims = (doms, snaps, me_d, me_s)
    left, right = (me_d + doms - 1) % doms, (me_d + 1) % doms
    halves = width // 128
    unit = halves * width
    red_a = Reduce(dims, 0, 4 * unit, part, fin, first_a, second_a, red[:6])
    red_b = Reduce(dims, 4 * unit, unit, part, fin, first_b, second_b, red[6:12])
    red_c = Reduce(dims, 5 * unit, unit, part, fin, first_c, second_c, red[12:])

    def put(n, value):
        for h in range(halves):
            part[pl.ds(n * unit + h * width, width), :] = value[:, h * 128 : (h + 1) * 128].astype(BF16)

    barrier = pltpu.get_barrier_semaphore()

    def greet(device):
        pl.semaphore_signal(
            barrier, inc=1, device_id=device, device_id_type=pl.DeviceIdType.MESH
        )

    greet((left, me_s))
    greet((right, me_s))
    for d in range(1, red_a.group):
        greet(red_a.member((red_a.mine + d) % red_a.group))
    for d in range(1, red_a.high):
        a = (red_a.hi + d) % red_a.high
        greet((a * red_a.low + me_d % red_a.low, me_s))
    pl.semaphore_wait(barrier, red_a.group + red_a.high)

    def to_right(s):
        return remote(feat.at[s], ext.at[s, pl.ds(0, HALO)], halo_s.at[0, s], halo_r.at[0, s], (right, me_s))

    def to_left(s):
        return remote(
            feat.at[s], ext.at[s, pl.ds(reach - HALO, HALO)], halo_s.at[1, s], halo_r.at[1, s], (left, me_s)
        )

    has_left, has_right = me_d > 0, me_d < doms - 1
    for s in range(local):
        pl.when(has_right)(lambda s=s: to_right(s).start())
        pl.when(has_left)(lambda s=s: to_left(s).start())

    def my_slots():
        return pl.ds(me_s * local, local)

    def share_of(p):
        return pl.ds(pl.multiple_of(p * share, share), share)

    cot_out = []
    for d in range(1, snaps):
        p = (me_s + d) % snaps
        copy = remote(
            cot.at[:, share_of(p)], cosw.at[my_slots()], cot_s.at[d - 1], cot_r.at[d - 1], (me_d, p)
        )
        copy.start()
        cot_out.append(copy)
    for s in range(local):
        cosw[me_s * local + s] = cot[s, share_of(me_s), :]

    @pl.when(jnp.logical_not(has_left))
    def _():
        ext[:, pl.ds(0, HALO), :] = jnp.zeros((local, HALO, width), BF16)
        ghl[...] = jnp.zeros(ghl.shape, BF16)

    @pl.when(jnp.logical_not(has_right))
    def _():
        ext[:, pl.ds(reach - HALO, HALO), :] = jnp.zeros((local, HALO, width), BF16)
        ghr[...] = jnp.zeros(ghr.shape, BF16)

    ext[:, pl.ds(HALO, nodes), :] = feat[...]

    first_row = me_d * nodes - HALO
    index = nb[...] - first_row
    index_t = jnp.concatenate([index] * (nodes // degree), axis=1).T
    lanes = lax.broadcasted_iota(jnp.int32, (nodes, reach), 1)
    subs = lax.broadcasted_iota(jnp.int32, (reach, nodes), 0)
    eye = jnp.where(
        lax.broadcasted_iota(jnp.int32, (nodes, nodes), 0)
        == lax.broadcasted_iota(jnp.int32, (nodes, nodes), 1),
        1.0,
        0.0,
    ).astype(BF16)
    counts = jnp.broadcast_to(deg[...], (nodes, nodes)).T
    inverse = 1.0 / counts.astype(F32)
    block = nodes // 2
    for j in range(degree):
        at = pl.ds(j * nodes, nodes)
        hit = jnp.where(lanes == index[:, j : j + 1], 1.0, 0.0).astype(BF16)
        for c in range(nodes // block):
            to = pl.ds((c * degree + j) * block, block)
            oh[to, pl.ds(0, reach)] = hit[c * block : (c + 1) * block]
            oh[to, pl.ds(reach, nodes)] = eye[c * block : (c + 1) * block]
        oht[pl.ds(0, reach), at] = jnp.where(subs == index_t[j : j + 1, :], 1.0, 0.0).astype(BF16)
        oht[pl.ds(reach, nodes), at] = eye
        wb[at, :] = jnp.where(counts > j, inverse, 0.0)

    spa_out = []
    for s in range(local):
        pl.when(has_left)(lambda s=s: to_right(s).wait_recv())
        pl.when(has_right)(lambda s=s: to_left(s).wait_recv())
        cat[pl.ds(0, reach), :] = dot(ext[s], wm[...]).astype(BF16)
        cat[pl.ds(reach, nodes), :] = feat[s]
        for c in range(nodes // block):
            before = dot(oh[pl.ds(c * degree * block, degree * block), :], cat[...])
            total = jnp.zeros((block, width), F32)
            for j in range(degree):
                at = pl.ds(j * nodes + c * block, block)
                x = before[j * block : (j + 1) * block]
                w = jnp.concatenate([wb[at, :]] * halves, axis=1)
                g = 0.5 * jnp.tanh(0.5 * x) + 0.5
                y = x * g
                total = total + w * y
                slope[s, at, :] = (w * (g + y * (1.0 - g))).astype(BF16)
            comb[s, pl.ds(c * block, block), :] = total.astype(BF16)
        spat[s] = (feat[s].astype(F32) + dot(comb[s], wc[...])).astype(BF16)
        for d in range(1, snaps):
            p = (me_s + d) % snaps
            copy = remote(
                spat.at[s, share_of(p)],
                spsw.at[me_s * local + s],
                spa_s.at[s, d - 1],
                spa_r.at[s, d - 1],
                (me_d, p),
            )
            copy.start()
            spa_out.append((s, d, copy))
        spsw[me_s * local + s] = spat[s, share_of(me_s), :]

    rows = SNAPS * share
    for copy in cot_out:
        copy.wait_recv()
    flat_cot = cosw[...].reshape(rows, width)
    ga[...] = dot_t(flat_cot, wo[...])
    for s, d, copy in spa_out:
        copy.wait_recv()
    flat_spat = spsw[...].reshape(rows, width)
    q[...] = dot(flat_spat, wa[:, 0:width])
    k[...] = dot(flat_spat, wa[:, width : 2 * width])
    v[...] = dot(flat_spat, wa[:, 2 * width : 3 * width])
    root = 1.0 / math.sqrt(HEAD_DIM)
    heads = jnp.where(
        lax.broadcasted_iota(jnp.int32, (width, width), 0) // HEAD_DIM
        == lax.broadcasted_iota(jnp.int32, (width, width), 1) // HEAD_DIM,
        1.0,
        0.0,
    ).astype(BF16)

    small = 16

    def attend(c, carry):
        def at(s):
            return pl.ds(pl.multiple_of(s * share + c * small, small), small)

        def piece(values, s, r):
            n = (s * SNAPS + r) * small
            return values[n : n + small]

        mines = [q[at(s), :] for s in range(SNAPS)]
        others = [ga[at(s), :] for s in range(SNAPS)]
        ks = [k[at(r), :] for r in range(SNAPS)]
        vs = [v[at(r), :] for r in range(SNAPS)]
        sc = dot(
            jnp.concatenate([(mines[s] * root * ks[r]).astype(BF16) for s in range(SNAPS) for r in range(SNAPS)]),
            heads,
        )
        gs = dot(
            jnp.concatenate([(others[s] * vs[r]).astype(BF16) for s in range(SNAPS) for r in range(SNAPS)]),
            heads,
        )
        gk_sum = [jnp.zeros((small, width), F32)] * SNAPS
        gv_sum = [jnp.zeros((small, width), F32)] * SNAPS
        for s in range(SNAPS):
            e = [jnp.exp(piece(sc, s, r)) for r in range(SNAPS)]
            norm = 1.0 / sum(e[1:], e[0])
            w = [x * norm for x in e]
            g = [piece(gs, s, r) for r in range(SNAPS)]
            prods = [x * y for x, y in zip(w, g)]
            mean = sum(prods[1:], prods[0])
            mine, other = mines[s], others[s]
            att_sum = jnp.zeros((small, width), F32)
            gq_sum = jnp.zeros((small, width), F32)
            for r in range(SNAPS):
                t = w[r] * (g[r] - mean)
                att_sum = att_sum + w[r] * vs[r]
                gq_sum = gq_sum + t * ks[r]
                gk_sum[r] = gk_sum[r] + t * mine
                gv_sum[r] = gv_sum[r] + w[r] * other
            att[at(s), :] = att_sum
            gq[at(s), :] = gq_sum * root
        for r in range(SNAPS):
            gk[at(r), :] = gk_sum[r] * root
            gv[at(r), :] = gv_sum[r]
        return carry

    lax.fori_loop(0, share // small, attend, 0)

    g3 = [gq[...].astype(BF16), gk[...].astype(BF16), gv[...].astype(BF16)]
    back = flat_cot.astype(F32)
    for n in range(3):
        back = back + dot_t(g3[n], wa[:, n * width : (n + 1) * width])
    gsw[...] = back.astype(BF16).reshape(SNAPS, share, width)
    gra_out = []
    for d in range(1, snaps):
        p = (me_s + d) % snaps
        copy = remote(
            gsw.at[pl.ds(p * local, local)],
            gsp.at[:, share_of(me_s)],
            gra_s.at[d - 1],
            gra_r.at[d - 1],
            (me_d, p),
        )
        copy.start()
        gra_out.append(copy)
    for s in range(local):
        gsp[s, share_of(me_s), :] = gsw[me_s * local + s]
    put(0, t_dot(att[...].astype(BF16), flat_cot))
    for n in range(3):
        put(n + 1, t_dot(flat_spat, g3[n]))
    red_a.start()
    for d in range(1, snaps):
        p = (me_s + snaps - d) % snaps
        remote(
            gsw.at[pl.ds(p * local, local)],
            gsp.at[:, share_of(p)],
            gra_s.at[d - 1],
            gra_r.at[d - 1],
            (me_d, p),
        ).wait_recv()

    def ghost_left(s):
        return remote(grow.at[s, pl.ds(0, HALO)], ghr.at[s], gho_s.at[0, s], gho_r.at[0, s], (left, me_s))

    def ghost_right(s):
        return remote(
            grow.at[s, pl.ds(reach - HALO, HALO)], ghl.at[s], gho_s.at[1, s], gho_r.at[1, s], (right, me_s)
        )

    put(
        4, t_dot(comb[...].reshape(local * nodes, width), gsp[...].reshape(local * nodes, width))
    )
    red_b.start()
    for s in range(local):
        gc = dot_t(gsp[s], wc[...])
        gb = jnp.concatenate(
            [(gc * slope[s, pl.ds(j * nodes, nodes), :].astype(F32)).astype(BF16) for j in range(degree)]
        )
        sums = dot(oht[...], gb)
        grow[s] = sums[:reach].astype(BF16)
        ownf[s] = sums[HALO : HALO + nodes]
        selff[s] = sums[reach:]
        pl.when(has_left)(lambda s=s: ghost_left(s).start())
        pl.when(has_right)(lambda s=s: ghost_right(s).start())
        if s == local // 2:
            red_a.middle()
    put(
        5, t_dot(ext[...].reshape(local * reach, width), grow[...].reshape(local * reach, width))
    )
    red_c.start()
    red_b.middle()
    red_a.spread()
    for s in range(local):
        pl.when(has_right)(lambda s=s: ghost_left(s).wait_recv())
        pl.when(has_left)(lambda s=s: ghost_right(s).wait_recv())
        if s == local // 2:
            red_c.middle()
        own = ownf[s] + ghl[s].astype(F32) + ghr[s].astype(F32)
        here = gsp[s].astype(F32) + selff[s] + dot_t(own.astype(BF16), wm[...])
        gfeat[s] = here.astype(BF16)
    red_b.spread()
    red_c.spread()
    red_a.finish()
    red_b.finish()
    red_c.finish()
    wout[...] = fin[...]
    for s in range(local):
        @pl.when(has_right)
        def _(s=s):
            to_right(s).wait_send()
            ghost_right(s).wait_send()

        @pl.when(has_left)
        def _(s=s):
            to_left(s).wait_send()
            ghost_left(s).wait_send()
    for copy in cot_out + [c for _, _, c in spa_out] + gra_out:
        copy.wait_send()


def finish(factor, gfeat, wout, features, message, combine, attend, output):
    features[...] = gfeat[...]
    width = message.shape[0]
    homes = ((output, 0), (attend, 0), (attend, width), (attend, 2 * width), (combine, 0), (message, 0))
    row = 0
    for ref, column in homes:
        for h in range(width // 128):
            ref[:, pl.ds(column + h * 128, 128)] = wout[pl.ds(row, width), :].astype(F32) * factor
            row += width


def body(doms, snaps, features, cotangent, neighbours, degrees, message_proj, combine_proj, attend_proj, output_proj):
    local, nodes, width = features.shape
    degree = neighbours.shape[1]
    reach = nodes + 2 * HALO
    share = nodes // snaps
    rows = SNAPS * share
    unit = width // 128 * width
    low = LOW if doms % LOW == 0 else 1
    high, group = doms // low, low * snaps
    dma = pltpu.SemaphoreType.DMA
    vmem = pltpu.VMEM

    def reduce_sems():
        g, h = (max(group - 1, 1),), (max(high - 1, 1),)
        return [dma(g), dma(g), dma(h), dma(h), dma(g), dma(g)]

    peers = max(snaps - 1, 1)
    gfeat, wout = pl.pallas_call(
        functools.partial(kernel, doms, snaps),
        out_shape=(
            jax.ShapeDtypeStruct(features.shape, BF16),
            jax.ShapeDtypeStruct((6 * unit, 128), BF16),
        ),
        in_specs=[pl.BlockSpec(memory_space=pltpu.VMEM)] * 8,
        out_specs=[pl.BlockSpec(memory_space=pltpu.VMEM)] * 2,
        scratch_shapes=[
            vmem((local, reach, width), BF16),
            vmem((reach + nodes, width), BF16),
            vmem((degree * nodes, reach + nodes), BF16),
            vmem((reach + nodes, degree * nodes), BF16),
            vmem((degree * nodes, 128), F32),
            vmem((local, degree * nodes, width), BF16),
            vmem((local, nodes, width), BF16),
            vmem((local, nodes, width), BF16),
            vmem((SNAPS, share, width), BF16),
            vmem((SNAPS, share, width), BF16),
            *[vmem((rows, width), F32)] * 8,
            vmem((SNAPS, share, width), BF16),
            vmem((local, nodes, width), BF16),
            vmem((local, reach, width), BF16),
            vmem((local, nodes, width), F32),
            vmem((local, nodes, width), F32),
            vmem((local, HALO, width), BF16),
            vmem((local, HALO, width), BF16),
            vmem((6 * unit, 128), BF16),
            *[
                vmem((count, size // group, 128), BF16)
                for size in (4 * unit, unit, unit)
                for count in (group - 1, high)
            ],
            vmem((6 * unit, 128), BF16),
            dma((2, local)),
            dma((2, local)),
            dma((2, local)),
            dma((2, local)),
            dma((peers,)),
            dma((peers,)),
            dma((local, peers)),
            dma((local, peers)),
            dma((peers,)),
            dma((peers,)),
            *reduce_sems(),
            *reduce_sems(),
            *reduce_sems(),
        ],
        compiler_params=pltpu.CompilerParams(
            collective_id=0, has_side_effects=True, vmem_limit_bytes=56 * 2**20
        ),
    )(
        features, cotangent, neighbours, degrees.reshape(1, nodes),
        message_proj, combine_proj, attend_proj, output_proj,
    )
    factor = 1.0 / math.sqrt(SNAPS * doms * nodes)
    square = jax.ShapeDtypeStruct((width, width), F32)
    return pl.pallas_call(
        functools.partial(finish, factor),
        out_shape=(
            jax.ShapeDtypeStruct(features.shape, BF16),
            square,
            square,
            jax.ShapeDtypeStruct((width, 3 * width), F32),
            square,
        ),
        in_specs=[pl.BlockSpec(memory_space=pltpu.VMEM)] * 2,
        out_specs=[pl.BlockSpec(memory_space=pltpu.VMEM)] * 5,
    )(gfeat, wout)


def solution(mesh):
    in_specs = (
        P("snap", "dom", None),
        P("snap", "dom", None),
        P("dom", None),
        P("dom"),
        P(),
        P(),
        P(),
        P(),
    )
    out_specs = (P("snap", "dom", None), P(), P(), P(), P())
    return jax.shard_map(
        functools.partial(body, mesh.shape["dom"], mesh.shape["snap"]),
        mesh=mesh,
        in_specs=in_specs,
        out_specs=out_specs,
        check_vma=False,
    )
```

```python
import functools
import math

import jax
import jax.numpy as jnp
from jax import lax
from jax.experimental import pallas as pl
from jax.experimental.pallas import tpu as pltpu
from jax.sharding import PartitionSpec as P

HEAD_DIM = 32
SNAPS = 8
HALO = 128
LOW = 4
F32 = jnp.float32
BF16 = jnp.bfloat16


def dot(a, b):
    return jnp.dot(a, b, preferred_element_type=F32)


def dot_t(a, b):
    return lax.dot_general(a, b, (((1,), (1,)), ((), ())), preferred_element_type=F32)


def t_dot(a, b):
    return lax.dot_general(a, b, (((0,), (0,)), ((), ())), preferred_element_type=F32)


def remote(src, dst, send, recv, device):
    return pltpu.make_async_remote_copy(
        src_ref=src,
        dst_ref=dst,
        send_sem=send,
        recv_sem=recv,
        device_id=device,
        device_id_type=pl.DeviceIdType.MESH,
    )


class Reduce:
    def __init__(self, dims, base, rows, part, fin, first, second, sems):
        self.doms, self.snaps, self.me_d, self.me_s = dims
        self.low = LOW if self.doms % LOW == 0 else 1
        self.high = self.doms // self.low
        self.group = self.low * self.snaps
        self.piece = rows // self.group
        self.base = base
        self.part, self.fin, self.first, self.second = part, fin, first, second
        self.sems = sems
        self.hi = self.me_d // self.low
        self.mine = self.me_s * self.low + self.me_d % self.low
        self.sent = []

    def member(self, t):
        return (self.hi * self.low + t % self.low, t // self.low)

    def rows_of(self, t):
        return pl.ds(pl.multiple_of(self.base + t * self.piece, 16), self.piece)

    def start(self):
        s1, r1 = self.sems[0], self.sems[1]
        for d in range(1, self.group):
            t = (self.mine + d) % self.group
            copy = remote(
                self.part.at[self.rows_of(t)],
                self.first.at[d - 1],
                s1.at[d - 1],
                r1.at[d - 1],
                self.member(t),
            )
            copy.start()
            self.sent.append(copy)
        self.one = list(self.sent)

    def middle(self):
        s2, r2 = self.sems[2], self.sems[3]
        total = self.part[self.rows_of(self.mine), :].astype(F32)
        for d in range(1, self.group):
            self.one[d - 1].wait_recv()
            total = total + self.first[d - 1].astype(F32)
        self.second[self.hi] = total.astype(BF16)
        for d in range(1, self.high):
            a = (self.hi + d) % self.high
            copy = remote(
                self.second.at[self.hi],
                self.second.at[self.hi],
                s2.at[d - 1],
                r2.at[d - 1],
                (a * self.low + self.me_d % self.low, self.me_s),
            )
            copy.start()
            self.sent.append(copy)

    def spread(self):
        s2, r2, s3, r3 = self.sems[2:]
        for d in range(1, self.high):
            a = (self.hi + self.high - d) % self.high
            remote(
                self.second.at[a],
                self.second.at[a],
                s2.at[d - 1],
                r2.at[d - 1],
                (a * self.low + self.me_d % self.low, self.me_s),
            ).wait_recv()
        total = self.second[0].astype(F32)
        for a in range(1, self.high):
            total = total + self.second[a].astype(F32)
        self.fin[self.rows_of(self.mine), :] = total.astype(BF16)
        for d in range(1, self.group):
            t = (self.mine + d) % self.group
            copy = remote(
                self.fin.at[self.rows_of(self.mine)],
                self.fin.at[self.rows_of(self.mine)],
                s3.at[d - 1],
                r3.at[d - 1],
                self.member(t),
            )
            copy.start()
            self.sent.append(copy)

    def finish(self):
        s3, r3 = self.sems[4:]
        for d in range(1, self.group):
            t = (self.mine + self.group - d) % self.group
            remote(
                self.fin.at[self.rows_of(t)],
                self.fin.at[self.rows_of(t)],
                s3.at[d - 1],
                r3.at[d - 1],
                self.member(t),
            ).wait_recv()
        for copy in self.sent:
            copy.wait_send()


def kernel(
    doms, snaps,
    feat, cot, nbt, deg, wm, wc, wa, wo,
    gfeat, wout,
    ext, cat, oh, oht, slope, comb, spat, spsw, cosw,
    q, k, v, ga, gq, gk, gv, att, gsw, gsp, grow, ownf, selff, ghl, ghr,
    part, first_a, second_a, first_b, second_b, first_c, second_c, fin,
    halo_s, halo_r, gho_s, gho_r, cot_s, cot_r, spa_s, spa_r, gra_s, gra_r, *red,
):
    local, nodes, width = feat.shape
    degree = nbt.shape[0]
    reach = nodes + 2 * HALO
    share = nodes // snaps
    me_d, me_s = lax.axis_index("dom"), lax.axis_index("snap")
    dims = (doms, snaps, me_d, me_s)
    left, right = (me_d + doms - 1) % doms, (me_d + 1) % doms
    halves = width // 128
    unit = halves * width
    red_a = Reduce(dims, 0, 4 * unit, part, fin, first_a, second_a, red[:6])
    red_b = Reduce(dims, 4 * unit, unit, part, fin, first_b, second_b, red[6:12])
    red_c = Reduce(dims, 5 * unit, unit, part, fin, first_c, second_c, red[12:])

    def put(n, value):
        for h in range(halves):
            part[pl.ds(n * unit + h * width, width), :] = value[:, h * 128 : (h + 1) * 128].astype(BF16)

    barrier = pltpu.get_barrier_semaphore()

    def greet(device):
        pl.semaphore_signal(
            barrier, inc=1, device_id=device, device_id_type=pl.DeviceIdType.MESH
        )

    greet((left, me_s))
    greet((right, me_s))
    for d in range(1, red_a.group):
        greet(red_a.member((red_a.mine + d) % red_a.group))
    for d in range(1, red_a.high):
        a = (red_a.hi + d) % red_a.high
        greet((a * red_a.low + me_d % red_a.low, me_s))
    pl.semaphore_wait(barrier, red_a.group + red_a.high)

    def to_right(s):
        return remote(feat.at[s], ext.at[s, pl.ds(0, HALO)], halo_s.at[0, s], halo_r.at[0, s], (right, me_s))

    def to_left(s):
        return remote(
            feat.at[s], ext.at[s, pl.ds(reach - HALO, HALO)], halo_s.at[1, s], halo_r.at[1, s], (left, me_s)
        )

    has_left, has_right = me_d > 0, me_d < doms - 1
    for s in range(local):
        pl.when(has_right)(lambda s=s: to_right(s).start())
        pl.when(has_left)(lambda s=s: to_left(s).start())

    def my_slots():
        return pl.ds(me_s * local, local)

    def share_of(p):
        return pl.ds(pl.multiple_of(p * share, share), share)

    cot_out = []
    for d in range(1, snaps):
        p = (me_s + d) % snaps
        copy = remote(
            cot.at[:, share_of(p)], cosw.at[my_slots()], cot_s.at[d - 1], cot_r.at[d - 1], (me_d, p)
        )
        copy.start()
        cot_out.append(copy)
    for s in range(local):
        cosw[me_s * local + s] = cot[s, share_of(me_s), :]

    @pl.when(jnp.logical_not(has_left))
    def _():
        ext[:, pl.ds(0, HALO), :] = jnp.zeros((local, HALO, width), BF16)
        ghl[...] = jnp.zeros(ghl.shape, BF16)

    @pl.when(jnp.logical_not(has_right))
    def _():
        ext[:, pl.ds(reach - HALO, HALO), :] = jnp.zeros((local, HALO, width), BF16)
        ghr[...] = jnp.zeros(ghr.shape, BF16)

    ext[:, pl.ds(HALO, nodes), :] = feat[...]

    first_row = me_d * nodes - HALO
    index_t = nbt[...] - first_row
    index = jnp.concatenate([index_t] * (nodes // degree), axis=0).T
    lanes = lax.broadcasted_iota(jnp.int32, (nodes, reach), 1)
    subs = lax.broadcasted_iota(jnp.int32, (reach, nodes), 0)
    same = lax.broadcasted_iota(jnp.int32, (nodes, nodes), 0) == lax.broadcasted_iota(
        jnp.int32, (nodes, nodes), 1
    )
    one = jnp.where(same, 1.0, 0.0)
    eye = one.astype(BF16)
    count_row = deg[...]
    counts = jnp.broadcast_to(count_row, (nodes, nodes)).T
    inverse = jnp.concatenate([1.0 / counts.astype(F32)] * (width // nodes), axis=1)
    block = nodes // 2
    for j in range(degree):
        at = pl.ds(j * nodes, nodes)
        hit = jnp.where(lanes == index[:, j : j + 1], 1.0, 0.0).astype(BF16)
        for c in range(nodes // block):
            to = pl.ds((c * degree + j) * block, block)
            oh[to, pl.ds(0, reach)] = hit[c * block : (c + 1) * block]
            oh[to, pl.ds(reach, nodes)] = eye[c * block : (c + 1) * block]
        used = count_row > j
        row = jnp.where(used, index_t[j : j + 1, :], -1)
        oht[pl.ds(0, reach), at] = jnp.where(subs == row, 1.0, 0.0).astype(BF16)
        oht[pl.ds(reach, nodes), at] = jnp.where(used, one, 0.0).astype(BF16)

    spa_out = []
    for s in range(local):
        pl.when(has_left)(lambda s=s: to_right(s).wait_recv())
        pl.when(has_right)(lambda s=s: to_left(s).wait_recv())
        cat[pl.ds(0, reach), :] = (0.5 * dot(ext[s], wm[...])).astype(BF16)
        cat[pl.ds(reach, nodes), :] = (0.5 * feat[s].astype(F32)).astype(BF16)
        messages = [None] * (degree * nodes // block)
        for c in range(nodes // block):
            before = dot(oh[pl.ds(c * degree * block, degree * block), :], cat[...])
            for j in range(degree):
                half = before[j * block : (j + 1) * block]
                t = jnp.tanh(half)
                u = 1.0 + t
                messages[j * (nodes // block) + c] = (half * u).astype(BF16)
                slope[s, pl.ds(j * nodes + c * block, block), :] = (u * (1.0 + half * (1.0 - t))).astype(BF16)
        total = dot(oht[pl.ds(reach, nodes), :], jnp.concatenate(messages))
        comb[s] = (total * inverse).astype(BF16)
        spat[s] = (feat[s].astype(F32) + dot(comb[s], wc[...])).astype(BF16)
        for d in range(1, snaps):
            p = (me_s + d) % snaps
            copy = remote(
                spat.at[s, share_of(p)],
                spsw.at[me_s * local + s],
                spa_s.at[s, d - 1],
                spa_r.at[s, d - 1],
                (me_d, p),
            )
            copy.start()
            spa_out.append((s, d, copy))
        spsw[me_s * local + s] = spat[s, share_of(me_s), :]

    rows = SNAPS * share
    for copy in cot_out:
        copy.wait_recv()
    flat_cot = cosw[...].reshape(rows, width)
    ga[...] = dot_t(flat_cot, wo[...])
    for s, d, copy in spa_out:
        copy.wait_recv()
    flat_spat = spsw[...].reshape(rows, width)
    q[...] = dot(flat_spat, wa[:, 0:width])
    k[...] = dot(flat_spat, wa[:, width : 2 * width])
    v[...] = dot(flat_spat, wa[:, 2 * width : 3 * width])
    root = 1.0 / math.sqrt(HEAD_DIM)
    heads = jnp.where(
        lax.broadcasted_iota(jnp.int32, (width, width), 0) // HEAD_DIM
        == lax.broadcasted_iota(jnp.int32, (width, width), 1) // HEAD_DIM,
        1.0,
        0.0,
    ).astype(BF16)

    small = 16

    def attend(c, carry):
        def at(s):
            return pl.ds(pl.multiple_of(s * share + c * small, small), small)

        def piece(values, s, r):
            n = (s * SNAPS + r) * small
            return values[n : n + small]

        mines = [q[at(s), :] for s in range(SNAPS)]
        others = [ga[at(s), :] for s in range(SNAPS)]
        ks = [k[at(r), :] for r in range(SNAPS)]
        vs = [v[at(r), :] for r in range(SNAPS)]
        sc = dot(
            jnp.concatenate([(mines[s] * root * ks[r]).astype(BF16) for s in range(SNAPS) for r in range(SNAPS)]),
            heads,
        )
        gs = dot(
            jnp.concatenate([(others[s] * vs[r]).astype(BF16) for s in range(SNAPS) for r in range(SNAPS)]),
            heads,
        )
        gk_sum = [jnp.zeros((small, width), F32)] * SNAPS
        gv_sum = [jnp.zeros((small, width), F32)] * SNAPS
        for s in range(SNAPS):
            e = [jnp.exp(piece(sc, s, r)) for r in range(SNAPS)]
            norm = 1.0 / sum(e[1:], e[0])
            w = [x * norm for x in e]
            g = [piece(gs, s, r) for r in range(SNAPS)]
            prods = [x * y for x, y in zip(w, g)]
            mean = sum(prods[1:], prods[0])
            mine, other = mines[s], others[s]
            att_sum = jnp.zeros((small, width), F32)
            gq_sum = jnp.zeros((small, width), F32)
            for r in range(SNAPS):
                t = w[r] * (g[r] - mean)
                att_sum = att_sum + w[r] * vs[r]
                gq_sum = gq_sum + t * ks[r]
                gk_sum[r] = gk_sum[r] + t * mine
                gv_sum[r] = gv_sum[r] + w[r] * other
            att[at(s), :] = att_sum
            gq[at(s), :] = gq_sum * root
        for r in range(SNAPS):
            gk[at(r), :] = gk_sum[r] * root
            gv[at(r), :] = gv_sum[r]
        return carry

    lax.fori_loop(0, share // small, attend, 0)

    g3 = [gq[...].astype(BF16), gk[...].astype(BF16), gv[...].astype(BF16)]
    back = flat_cot.astype(F32)
    for n in range(3):
        back = back + dot_t(g3[n], wa[:, n * width : (n + 1) * width])
    gsw[...] = back.astype(BF16).reshape(SNAPS, share, width)
    gra_out = []
    for d in range(1, snaps):
        p = (me_s + d) % snaps
        copy = remote(
            gsw.at[pl.ds(p * local, local)],
            gsp.at[:, share_of(me_s)],
            gra_s.at[d - 1],
            gra_r.at[d - 1],
            (me_d, p),
        )
        copy.start()
        gra_out.append(copy)
    for s in range(local):
        gsp[s, share_of(me_s), :] = gsw[me_s * local + s]
    put(0, t_dot(att[...].astype(BF16), flat_cot))
    for n in range(3):
        put(n + 1, t_dot(flat_spat, g3[n]))
    red_a.start()
    for d in range(1, snaps):
        p = (me_s + snaps - d) % snaps
        remote(
            gsw.at[pl.ds(p * local, local)],
            gsp.at[:, share_of(p)],
            gra_s.at[d - 1],
            gra_r.at[d - 1],
            (me_d, p),
        ).wait_recv()

    def ghost_left(s):
        return remote(grow.at[s, pl.ds(0, HALO)], ghr.at[s], gho_s.at[0, s], gho_r.at[0, s], (left, me_s))

    def ghost_right(s):
        return remote(
            grow.at[s, pl.ds(reach - HALO, HALO)], ghl.at[s], gho_s.at[1, s], gho_r.at[1, s], (right, me_s)
        )

    put(
        4, t_dot(comb[...].reshape(local * nodes, width), gsp[...].reshape(local * nodes, width))
    )
    red_b.start()
    for s in range(local):
        gc = (dot_t(gsp[s], wc[...]) * (0.5 * inverse)).astype(BF16)
        gb = jnp.concatenate([gc * slope[s, pl.ds(j * nodes, nodes), :] for j in range(degree)])
        sums = dot(oht[...], gb)
        grow[s] = sums[:reach].astype(BF16)
        ownf[s] = sums[HALO : HALO + nodes]
        selff[s] = sums[reach:]
        pl.when(has_left)(lambda s=s: ghost_left(s).start())
        pl.when(has_right)(lambda s=s: ghost_right(s).start())
        if s == local // 2:
            red_a.middle()
    put(
        5, t_dot(ext[...].reshape(local * reach, width), grow[...].reshape(local * reach, width))
    )
    red_c.start()
    red_b.middle()
    for s in range(local):
        pl.when(has_right)(lambda s=s: ghost_left(s).wait_recv())
        pl.when(has_left)(lambda s=s: ghost_right(s).wait_recv())
        own = ownf[s] + ghl[s].astype(F32) + ghr[s].astype(F32)
        here = gsp[s].astype(F32) + selff[s] + dot_t(own.astype(BF16), wm[...])
        gfeat[s] = here.astype(BF16)
    red_c.middle()
    red_a.spread()
    red_b.spread()
    red_c.spread()
    red_a.finish()
    red_b.finish()
    red_c.finish()
    wout[...] = fin[...]
    for s in range(local):
        @pl.when(has_right)
        def _(s=s):
            to_right(s).wait_send()
            ghost_right(s).wait_send()

        @pl.when(has_left)
        def _(s=s):
            to_left(s).wait_send()
            ghost_left(s).wait_send()
    for copy in cot_out + [c for _, _, c in spa_out] + gra_out:
        copy.wait_send()


def finish(factor, gfeat, wout, features, message, combine, attend, output):
    features[...] = gfeat[...]
    width = message.shape[0]
    homes = ((output, 0), (attend, 0), (attend, width), (attend, 2 * width), (combine, 0), (message, 0))
    row = 0
    for ref, column in homes:
        for h in range(width // 128):
            ref[:, pl.ds(column + h * 128, 128)] = wout[pl.ds(row, width), :].astype(F32) * factor
            row += width


def body(doms, snaps, features, cotangent, neighbours, degrees, message_proj, combine_proj, attend_proj, output_proj):
    local, nodes, width = features.shape
    degree = neighbours.shape[1]
    reach = nodes + 2 * HALO
    share = nodes // snaps
    rows = SNAPS * share
    unit = width // 128 * width
    low = LOW if doms % LOW == 0 else 1
    high, group = doms // low, low * snaps
    dma = pltpu.SemaphoreType.DMA
    vmem = pltpu.VMEM

    def reduce_sems():
        g, h = (max(group - 1, 1),), (max(high - 1, 1),)
        return [dma(g), dma(g), dma(h), dma(h), dma(g), dma(g)]

    peers = max(snaps - 1, 1)
    gfeat, wout = pl.pallas_call(
        functools.partial(kernel, doms, snaps),
        out_shape=(
            jax.ShapeDtypeStruct(features.shape, BF16),
            jax.ShapeDtypeStruct((6 * unit, 128), BF16),
        ),
        in_specs=[pl.BlockSpec(memory_space=pltpu.VMEM)] * 8,
        out_specs=[pl.BlockSpec(memory_space=pltpu.VMEM)] * 2,
        scratch_shapes=[
            vmem((local, reach, width), BF16),
            vmem((reach + nodes, width), BF16),
            vmem((degree * nodes, reach + nodes), BF16),
            vmem((reach + nodes, degree * nodes), BF16),
            vmem((local, degree * nodes, width), BF16),
            vmem((local, nodes, width), BF16),
            vmem((local, nodes, width), BF16),
            vmem((SNAPS, share, width), BF16),
            vmem((SNAPS, share, width), BF16),
            *[vmem((rows, width), F32)] * 8,
            vmem((SNAPS, share, width), BF16),
            vmem((local, nodes, width), BF16),
            vmem((local, reach, width), BF16),
            vmem((local, nodes, width), F32),
            vmem((local, nodes, width), F32),
            vmem((local, HALO, width), BF16),
            vmem((local, HALO, width), BF16),
            vmem((6 * unit, 128), BF16),
            *[
                vmem((count, size // group, 128), BF16)
                for size in (4 * unit, unit, unit)
                for count in (group - 1, high)
            ],
            vmem((6 * unit, 128), BF16),
            dma((2, local)),
            dma((2, local)),
            dma((2, local)),
            dma((2, local)),
            dma((peers,)),
            dma((peers,)),
            dma((local, peers)),
            dma((local, peers)),
            dma((peers,)),
            dma((peers,)),
            *reduce_sems(),
            *reduce_sems(),
            *reduce_sems(),
        ],
        compiler_params=pltpu.CompilerParams(
            collective_id=0, has_side_effects=True, vmem_limit_bytes=56 * 2**20
        ),
    )(
        features, cotangent, neighbours.T, degrees.reshape(1, nodes),
        message_proj, combine_proj, attend_proj, output_proj,
    )
    factor = 1.0 / math.sqrt(SNAPS * doms * nodes)
    square = jax.ShapeDtypeStruct((width, width), F32)
    return pl.pallas_call(
        functools.partial(finish, factor),
        out_shape=(
            jax.ShapeDtypeStruct(features.shape, BF16),
            square,
            square,
            jax.ShapeDtypeStruct((width, 3 * width), F32),
            square,
        ),
        in_specs=[pl.BlockSpec(memory_space=pltpu.VMEM)] * 2,
        out_specs=[pl.BlockSpec(memory_space=pltpu.VMEM)] * 5,
    )(gfeat, wout)


def solution(mesh):
    in_specs = (
        P("snap", "dom", None),
        P("snap", "dom", None),
        P("dom", None),
        P("dom"),
        P(),
        P(),
        P(),
        P(),
    )
    out_specs = (P("snap", "dom", None), P(), P(), P(), P())
    return jax.shard_map(
        functools.partial(body, mesh.shape["dom"], mesh.shape["snap"]),
        mesh=mesh,
        in_specs=in_specs,
        out_specs=out_specs,
        check_vma=False,
    )
```
